32 devices in a mesh: ctx: 8 (over z, y), uly: 4 (over x, core).
Axes of the slice: x: 2, y: 2, z: 4, core: 2. Of those that a mesh axis runs over, the one named last changes fastest.
Arguments:
- queries: bfloat16 [8192, 4096], P(('ctx', 'uly')), may hold values from -12 to 12
- key_rows: bfloat16 [8192, 2048], P(('ctx', 'uly')), may hold values from -12 to 12
- value_rows: bfloat16 [8192, 2048], P(('ctx', 'uly')), may hold values from -6 to 6
- doc_lengths: int32 [8], replicated, may hold values from 1 to 2048, 8192 in all
Outputs:
- attended: bfloat16 [8192, 4096], P(('ctx', 'uly'))
The draws below stay inside these ranges and needn't reach their ends.
Inputs may be any that keep to these rules, and one draw needn't show every extreme that they name: `doc_lengths`: the 8 documents are packed in order and their lengths sum to 8192; the longest is exactly 2048.
All inputs are finite; a program needn't handle non-finite values.
Results may differ from the reference program's by a relative error of at most 0.005.
Values may be sent and summed in bfloat16 or wider, within the bound.
A program may use at most 64 MiB of HBM per device.

```python
import math
import jax
import jax.numpy as jnp
import numpy as np
from jax import lax

HQ = 32
HK = 16
HD = 128
TOKENS = 8192
MOST = 2048
NDOCS = 8


def shard_levels(own_key, dims, shards, low, largest):
    factor_of = 1.0
    for dim, shards_of in shards:
        steps = jax.random.uniform(jax.random.fold_in(jax.random.fold_in(own_key, 6), dim), (shards_of,), jnp.float32, low / len(shards), largest / len(shards))
        factor_of = factor_of * jnp.repeat(jnp.exp(steps), dims[dim] // shards_of).reshape((-1,) + (1,) * (len(dims) - 1 - dim))
    return factor_of


def profile(amount, total, limit, slope):
    loads = [(1 << 20) // math.isqrt(rank ** slope) + 1 for rank in range(2, amount + 1)]
    rest, holding = total - limit - (amount - 1), [1] * (amount - 1)
    while rest > 0:
        candidates = [i for i in range(amount - 1) if holding[i] < limit]
        pool, left = sum([loads[i] for i in candidates]), rest
        for i in candidates:
            more = min(limit - holding[i], max(1, left * loads[i] // pool), rest)
            holding[i] = holding[i] + more
            rest = rest - more
    return np.array([limit] + holding)


def uneven(stream_key, number_of, total, bound, lean):
    if number_of == 2:
        one = jax.random.randint(stream_key, (), max(1, total - bound), min(bound, total - 1) + 1)
        return jnp.stack([one, total - one])
    sizes = jnp.asarray(profile(number_of, total, bound, lean), jnp.int32)
    pairs = (number_of - 1) // 2
    giver, taker = sizes[1:1 + 2 * pairs:2], sizes[2:2 + 2 * pairs:2]
    slack = jnp.minimum(giver - 1, bound - taker)
    shifted = jax.random.randint(jax.random.fold_in(stream_key, 1), (pairs,), 0, 1 << 20) % (slack + 1)
    sizes = sizes.at[1:1 + 2 * pairs:2].set(giver - shifted).at[2:2 + 2 * pairs:2].set(taker + shifted)
    return sizes[jax.random.permutation(jax.random.fold_in(stream_key, 2), number_of)]


def centred(own_key, dims, spread, limit, shards=(), kind=jnp.bfloat16):
    factor_of = shard_levels(own_key, dims, shards, -0.22, 0.18) if shards else 1.0
    values = jax.random.normal(own_key, dims, jnp.float32) * spread * factor_of
    return jnp.minimum(jnp.maximum(values, -limit), limit).astype(kind)


def setup_inputs(seed: int = 0) -> dict:
    streams_of = jax.random.split(jax.random.key(seed), 5)
    queries = centred(streams_of[0], (TOKENS, HQ * HD), 2.0, 12.0, ((0, 32),))
    key_rows = centred(streams_of[1], (TOKENS, HK * HD), 2.0, 12.0, ((0, 32),))
    value_rows = centred(streams_of[2], (TOKENS, HK * HD), 1.0, 6.0, ((0, 32),))
    doc_lengths = uneven(streams_of[3], NDOCS, TOKENS, MOST, 2).astype(jnp.int32)
    return {"queries": queries, "key_rows": key_rows, "value_rows": value_rows, "doc_lengths": doc_lengths}


query_scale = 144.0 ** -0.5
logit_cap = 50.0


def doc_index(doc_lengths, positions):
    doc_ends = jnp.cumsum(doc_lengths, dtype=jnp.int32)
    return jnp.sum((doc_ends[None, :] <= positions[:, None]).astype(jnp.int32), axis=1, dtype=jnp.int32)


def reference(queries, key_rows, value_rows, doc_lengths):
    positions = jnp.arange(TOKENS, dtype=jnp.int32)
    doc_ids = doc_index(doc_lengths, positions)
    block_rows = min(512, MOST)
    window = MOST + block_rows
    zero_keys = jnp.zeros((MOST, HK * HD), key_rows.dtype)
    zero_values = jnp.zeros((MOST, HK * HD), value_rows.dtype)
    padded_keys = jnp.concatenate([zero_keys, key_rows], axis=0)
    padded_values = jnp.concatenate([zero_values, value_rows], axis=0)
    key_places = jnp.arange(TOKENS + MOST, dtype=jnp.int32) - MOST
    key_groups = jnp.concatenate([jnp.full((MOST,), -1, jnp.int32), doc_ids])

    def one_block(block_index):
        first_pos = (block_index * block_rows).astype(jnp.int32)
        query_block = lax.dynamic_slice_in_dim(queries, first_pos, block_rows, 0).astype(jnp.float32)
        query_block = query_block.reshape(block_rows, HK, 2, HD)
        key_block = lax.dynamic_slice_in_dim(padded_keys, first_pos, window, 0).astype(jnp.float32)
        key_block = key_block.reshape(window, HK, HD)
        value_block = lax.dynamic_slice_in_dim(padded_values, first_pos, window, 0).astype(jnp.float32)
        value_block = value_block.reshape(window, HK, HD)
        key_place = lax.dynamic_slice_in_dim(key_places, first_pos, window, 0)
        key_group = lax.dynamic_slice_in_dim(key_groups, first_pos, window, 0)
        query_place = lax.dynamic_slice_in_dim(positions, first_pos, block_rows, 0)
        query_group = lax.dynamic_slice_in_dim(doc_ids, first_pos, block_rows, 0)
        scores = jnp.einsum("rhgd,shd->hgrs", query_block, key_block, precision=lax.Precision.HIGHEST)
        capped = logit_cap * jnp.tanh(scores * query_scale / logit_cap)
        allowed = (key_group[None, :] == query_group[:, None]) & (key_place[None, :] <= query_place[:, None])
        weights = jnp.where(allowed[None, None], jnp.exp(capped), 0.0)
        row_total = jnp.sum(weights, axis=-1)
        rounded = lax.optimization_barrier(weights.astype(jnp.bfloat16)).astype(jnp.float32)
        numerator = jnp.einsum("hgrs,shd->rhgd", rounded, value_block, precision=lax.Precision.HIGHEST)
        result = numerator / jnp.transpose(row_total, (2, 0, 1))[..., None]
        return result.reshape(block_rows, HQ * HD).astype(jnp.bfloat16)

    stacked = lax.map(one_block, jnp.arange(TOKENS // block_rows, dtype=jnp.int32))
    return stacked.reshape(TOKENS, HQ * HD)
```

```python
import functools
import math

import jax
import jax.numpy as jnp
from jax import lax
from jax.experimental import pallas as pl
from jax.experimental.pallas import tpu as pltpu
from jax.sharding import PartitionSpec as P

HD = 128
SPAN = 2
MESH = pl.DeviceIdType.MESH
SCALE = 144.0 ** (-0.5) / 50.0
CAP = 50.0 * math.log2(math.e)


def kernel(
    n_ctx, n_uly, lens_ref, q_ref, k_ref, v_ref, out_ref,
    q_all, k_all, v_all, out_buf, starts, acc, total,
    own_sem, kv_send, kv_recv, q_send, q_recv, halo_send, halo_recv, out_send, out_recv,
):
    size = SPAN * n_uly
    groups = n_ctx // SPAN
    rows = q_ref.shape[0]
    kv_cols = k_ref.shape[1] // size
    q_cols = q_ref.shape[1] // size
    kv_heads = kv_cols // HD
    share = q_cols // kv_cols
    me = lax.axis_index("ctx") * n_uly + lax.axis_index("uly")
    group, rank = me // size, me % size
    has_next = group < groups - 1
    has_prev = group > 0

    def device(g, r):
        flat = g * size + r
        return (flat // n_uly, flat % n_uly)

    def cols(r, width):
        return pl.ds(pl.multiple_of(r * width, width), width)

    barrier = pltpu.get_barrier_semaphore()
    for d in range(1, size):
        pl.semaphore_signal(barrier, inc=1, device_id=device(group, (rank + d) % size), device_id_type=MESH)

    @pl.when(has_next)
    def _():
        pl.semaphore_signal(barrier, inc=1, device_id=device(group + 1, rank), device_id_type=MESH)

    @pl.when(has_prev)
    def _():
        pl.semaphore_signal(barrier, inc=1, device_id=device(group - 1, rank), device_id_type=MESH)

    pl.semaphore_wait(barrier, size - 1 + jnp.where(has_next, 1, 0) + jnp.where(has_prev, 1, 0))

    def kv_copy(d):
        peer = (rank + d) % size
        return [
            pltpu.make_async_remote_copy(
                src_ref=src.at[:, cols(peer, kv_cols)],
                dst_ref=dst.at[size + rank],
                send_sem=kv_send.at[n, peer],
                recv_sem=kv_recv.at[n, rank],
                device_id=device(group, peer),
                device_id_type=MESH,
            )
            for n, (src, dst) in enumerate(((k_ref, k_all), (v_ref, v_all)))
        ]

    def q_copy(peer):
        return pltpu.make_async_remote_copy(
            src_ref=q_ref.at[:, cols(peer, q_cols)],
            dst_ref=q_all.at[rank],
            send_sem=q_send.at[peer],
            recv_sem=q_recv.at[rank],
            device_id=device(group, peer),
            device_id_type=MESH,
        )

    def halo_copy(s):
        return [
            pltpu.make_async_remote_copy(
                src_ref=buf.at[size + s],
                dst_ref=buf.at[s],
                send_sem=halo_send.at[n, s],
                recv_sem=halo_recv.at[n, s],
                device_id=device(group + 1, rank),
                device_id_type=MESH,
            )
            for n, buf in enumerate((k_all, v_all))
        ]

    def out_copy(i):
        return pltpu.make_async_remote_copy(
            src_ref=out_buf.at[i],
            dst_ref=out_ref.at[:, cols(rank, q_cols)],
            send_sem=out_send.at[i],
            recv_sem=out_recv.at[rank],
            device_id=device(group, i),
            device_id_type=MESH,
        )

    def arrived(dst, sem):
        pltpu.make_async_copy(dst, dst, sem).wait()

    for d in range(1, size):
        for copy in kv_copy(d):
            copy.start()
    own = [
        pltpu.make_async_copy(k_ref.at[:, cols(rank, kv_cols)], k_all.at[size + rank], own_sem.at[0]),
        pltpu.make_async_copy(v_ref.at[:, cols(rank, kv_cols)], v_all.at[size + rank], own_sem.at[1]),
        pltpu.make_async_copy(q_ref.at[:, cols(rank, q_cols)], q_all.at[rank], own_sem.at[2]),
    ]
    for copy in own:
        copy.start()

    origin = (group - 1) * size * rows

    def find_starts(i, _):
        positions = group * size * rows + i * rows + lax.broadcasted_iota(jnp.int32, (rows, HD), 0)

        def next_doc(n, carry):
            begin, found = carry
            return begin + lens_ref[n], jnp.where(begin <= positions, begin, found)

        _, found = lax.fori_loop(
            0, lens_ref.shape[0], next_doc, (jnp.int32(0), jnp.zeros((rows, HD), jnp.int32))
        )
        starts[i] = found - origin
        return 0

    lax.fori_loop(0, size, find_starts, 0)

    for copy in own:
        copy.wait()
    for d in range(size):
        source = (rank + size - d) % size
        if d:
            for n, buf in enumerate((k_all, v_all)):
                arrived(buf.at[size + source], kv_recv.at[n, source])

        @pl.when(has_next)
        def _():
            for copy in halo_copy(source):
                copy.start()

        if d:
            q_copy((rank + d) % size).start()

    def block(i, slot, causal, first):
        begin = starts[i] - slot * rows
        begin = jnp.concatenate([begin] * (rows // HD), axis=1)
        place = lax.broadcasted_iota(jnp.int32, (rows, rows), 1)
        allowed = place >= begin
        if causal:
            allowed = allowed & (place <= lax.broadcasted_iota(jnp.int32, (rows, rows), 0))
        for h in range(kv_heads):
            key = k_all[slot, :, h * HD:(h + 1) * HD]
            value = v_all[slot, :, h * HD:(h + 1) * HD]
            for j in range(h * share, (h + 1) * share):
                query = q_all[i, :, j * HD:(j + 1) * HD]
                scores = lax.dot_general(
                    query, key, (((1,), (1,)), ((), ())), preferred_element_type=jnp.float32
                )
                weights = jnp.where(allowed, jnp.exp2(jnp.tanh(scores * SCALE) * CAP), 0.0)
                part = sum(weights[:, c * HD:(c + 1) * HD] for c in range(rows // HD))
                product = jnp.dot(
                    weights.astype(jnp.bfloat16), value, preferred_element_type=jnp.float32
                )
                if first:
                    total[i, j] = part
                    acc[i, j] = product
                else:
                    total[i, j] += part
                    acc[i, j] += product

    def own_part(i, _):
        @pl.when(i != rank)
        def _():
            arrived(q_all.at[i], q_recv.at[i])

        block(i, size + i, True, True)

        def step(j, _):
            block(i, size + j, False, False)
            return 0

        lax.fori_loop(0, i, step, 0)
        return 0

    lax.fori_loop(0, size, own_part, 0)

    def halo_part(n, _):
        i = size - 1 - n

        @pl.when(has_prev)
        def _():
            for m, buf in enumerate((k_all, v_all)):
                arrived(buf.at[i], halo_recv.at[m, i])

        def step(j, _):
            block(i, j, False, False)
            return 0

        lax.fori_loop(i, jnp.where(has_prev, size, 0), step, 0)
        for j in range(kv_heads * share):
            row_total = jnp.sum(total[i, j], axis=1, keepdims=True)
            out_buf[i, :, j * HD:(j + 1) * HD] = (acc[i, j] / row_total).astype(jnp.bfloat16)

        @pl.when(i != rank)
        def _():
            out_copy(i).start()

        @pl.when(i == rank)
        def _():
            pltpu.make_async_copy(out_buf.at[i], out_ref.at[:, cols(rank, q_cols)], own_sem.at[0]).start()

        return 0

    lax.fori_loop(0, size, halo_part, 0)

    pltpu.make_async_copy(out_buf.at[rank], out_ref.at[:, cols(rank, q_cols)], own_sem.at[0]).wait()
    for d in range(1, size):
        peer = (rank + d) % size
        for copy in kv_copy(d):
            copy.wait_send()
        q_copy(peer).wait_send()
        out_copy(peer).wait_send()
        arrived(out_ref.at[:, cols(peer, q_cols)], out_recv.at[peer])

    @pl.when(has_next)
    def _():
        for s in range(size):
            for copy in halo_copy(s):
                copy.wait_send()


def shards(n_ctx, n_uly, queries, key_rows, value_rows, doc_lengths):
    size = SPAN * n_uly
    rows, q_width = queries.shape
    kv_cols, q_cols = key_rows.shape[1] // size, q_width // size
    heads = q_cols // HD
    dma = pltpu.SemaphoreType.DMA
    return pl.pallas_call(
        functools.partial(kernel, n_ctx, n_uly),
        out_shape=jax.ShapeDtypeStruct(queries.shape, jnp.bfloat16),
        in_specs=[pl.BlockSpec(memory_space=pltpu.SMEM)] + [pl.BlockSpec(memory_space=pl.ANY)] * 3,
        out_specs=pl.BlockSpec(memory_space=pl.ANY),
        scratch_shapes=[
            pltpu.VMEM((size, rows, q_cols), jnp.bfloat16),
            pltpu.VMEM((2 * size, rows, kv_cols), jnp.bfloat16),
            pltpu.VMEM((2 * size, rows, kv_cols), jnp.bfloat16),
            pltpu.VMEM((size, rows, q_cols), jnp.bfloat16),
            pltpu.VMEM((size, rows, HD), jnp.int32),
            pltpu.VMEM((size, heads, rows, HD), jnp.float32),
            pltpu.VMEM((size, heads, rows, HD), jnp.float32),
            dma((3,)),
            dma((2, size)),
            dma((2, size)),
            dma((size,)),
            dma((size,)),
            dma((2, size)),
            dma((2, size)),
            dma((size,)),
            dma((size,)),
        ],
        compiler_params=pltpu.CompilerParams(
            collective_id=0, has_side_effects=True, vmem_limit_bytes=48 * 1024 * 1024
        ),
    )(doc_lengths, queries, key_rows, value_rows)


def solution(mesh):
    placed = (P(("ctx", "uly"), None), P(("ctx", "uly"), None), P(("ctx", "uly"), None), P())
    return jax.shard_map(
        functools.partial(shards, mesh.shape["ctx"], mesh.shape["uly"]),
        mesh=mesh, in_specs=placed, out_specs=P(("ctx", "uly"), None), check_vma=False,
    )
```

```python
import functools
import math

import jax
import jax.numpy as jnp
from jax import lax
from jax.experimental import pallas as pl
from jax.experimental.pallas import tpu as pltpu
from jax.sharding import PartitionSpec as P

HD = 128
SPAN = 2
MESH = pl.DeviceIdType.MESH
SCALE = 144.0 ** (-0.5) / 50.0
CAP = 50.0 * math.log2(math.e)


def kernel(
    n_ctx, n_uly, lens_ref, q_ref, k_ref, v_ref, out_ref,
    q_all, k_all, v_all, out_buf, starts, acc, total,
    own_sem, kv_send, kv_recv, q_send, q_recv, halo_send, halo_recv, out_send, out_recv,
):
    size = SPAN * n_uly
    groups = n_ctx // SPAN
    rows = q_ref.shape[0]
    kv_cols = k_ref.shape[1] // size
    q_cols = q_ref.shape[1] // size
    kv_heads = kv_cols // HD
    share = q_cols // kv_cols
    width = share * HD
    me = lax.axis_index("ctx") * n_uly + lax.axis_index("uly")
    group, rank = me // size, me % size
    has_next = group < groups - 1
    has_prev = group > 0

    def device(g, r):
        flat = g * size + r
        return (flat // n_uly, flat % n_uly)

    def cols(r, width):
        return pl.ds(pl.multiple_of(r * width, width), width)

    barrier = pltpu.get_barrier_semaphore()
    for d in range(1, size):
        pl.semaphore_signal(barrier, inc=1, device_id=device(group, (rank + d) % size), device_id_type=MESH)

    @pl.when(has_next)
    def _():
        pl.semaphore_signal(barrier, inc=1, device_id=device(group + 1, rank), device_id_type=MESH)

    @pl.when(has_prev)
    def _():
        pl.semaphore_signal(barrier, inc=1, device_id=device(group - 1, rank), device_id_type=MESH)

    pl.semaphore_wait(barrier, size - 1 + jnp.where(has_next, 1, 0) + jnp.where(has_prev, 1, 0))

    def kv_copy(h, peer):
        return [
            pltpu.make_async_remote_copy(
                src_ref=src.at[:, cols(peer * kv_heads + h, HD)],
                dst_ref=dst.at[h, size + rank],
                send_sem=kv_send.at[n, h, peer],
                recv_sem=kv_recv.at[n, h, rank],
                device_id=device(group, peer),
                device_id_type=MESH,
            )
            for n, (src, dst) in enumerate(((k_ref, k_all), (v_ref, v_all)))
        ]

    def q_copy(h, peer):
        return pltpu.make_async_remote_copy(
            src_ref=q_ref.at[:, cols(peer * kv_heads + h, width)],
            dst_ref=q_all.at[h, rank],
            send_sem=q_send.at[h, peer],
            recv_sem=q_recv.at[h, rank],
            device_id=device(group, peer),
            device_id_type=MESH,
        )

    def halo_copy(h, s):
        return [
            pltpu.make_async_remote_copy(
                src_ref=buf.at[h, size + s],
                dst_ref=buf.at[h, s],
                send_sem=halo_send.at[n, h, s],
                recv_sem=halo_recv.at[n, h, s],
                device_id=device(group + 1, rank),
                device_id_type=MESH,
            )
            for n, buf in enumerate((k_all, v_all))
        ]

    def out_copy(h, i):
        return pltpu.make_async_remote_copy(
            src_ref=out_buf.at[h, i],
            dst_ref=out_ref.at[:, cols(rank * kv_heads + h, width)],
            send_sem=out_send.at[h, i],
            recv_sem=out_recv.at[h, rank],
            device_id=device(group, i),
            device_id_type=MESH,
        )

    def own_out(h):
        return pltpu.make_async_copy(
            out_buf.at[h, rank], out_ref.at[:, cols(rank * kv_heads + h, width)], own_sem.at[0, h]
        )

    def arrived(dst, sem):
        pltpu.make_async_copy(dst, dst, sem).wait()

    def kv_arrived(h, source):
        for n, buf in enumerate((k_all, v_all)):
            arrived(buf.at[h, size + source], kv_recv.at[n, h, source])

    def forward(h, source):
        @pl.when(has_next)
        def _():
            for copy in halo_copy(h, source):
                copy.start()

    for d in range(1, size):
        for copy in kv_copy(0, (rank + d) % size):
            copy.start()
    for d in range(1, size):
        q_copy(0, (rank + d) % size).start()
    own = []
    for h in range(kv_heads):
        for n, (src, dst) in enumerate(((k_ref, k_all), (v_ref, v_all))):
            own.append(pltpu.make_async_copy(
                src.at[:, cols(rank * kv_heads + h, HD)], dst.at[h, size + rank], own_sem.at[n, h]
            ))
        own.append(pltpu.make_async_copy(
            q_ref.at[:, cols(rank * kv_heads + h, width)], q_all.at[h, rank], own_sem.at[2, h]
        ))
    for copy in own:
        copy.start()

    origin = (group - 1) * size * rows

    def find_starts(i, _):
        positions = group * size * rows + i * rows + lax.broadcasted_iota(jnp.int32, (rows, HD), 0)

        def next_doc(n, carry):
            begin, found = carry
            return begin + lens_ref[n], jnp.where(begin <= positions, begin, found)

        _, found = lax.fori_loop(
            0, lens_ref.shape[0], next_doc, (jnp.int32(0), jnp.zeros((rows, HD), jnp.int32))
        )
        starts[i] = found - origin
        return 0

    lax.fori_loop(0, size, find_starts, 0)

    for copy in own:
        copy.wait()
    for d in range(size):
        source = (rank + size - d) % size
        if d:
            kv_arrived(0, source)
        forward(0, source)
        if d:
            for h in range(1, kv_heads):
                for copy in kv_copy(h, (rank + d) % size):
                    copy.start()

    def block(h, i, slot, count, first):
        keys = count * rows
        begin = starts[i] - slot * rows
        begin = jnp.concatenate([begin] * (keys // HD), axis=1)
        place = lax.broadcasted_iota(jnp.int32, (rows, keys), 1)
        allowed = place >= begin
        if first:
            allowed = allowed & (place <= lax.broadcasted_iota(jnp.int32, (rows, keys), 0))
        key = k_all[h, pl.ds(slot, count)].reshape(keys, HD)
        value = v_all[h, pl.ds(slot, count)].reshape(keys, HD)
        for j in range(share):
            query = q_all[h, i, :, j * HD:(j + 1) * HD]
            scores = lax.dot_general(
                query, key, (((1,), (1,)), ((), ())), preferred_element_type=jnp.float32
            )
            weights = jnp.where(allowed, jnp.exp2(jnp.tanh(scores * SCALE) * CAP), 0.0)
            part = sum(weights[:, c * HD:(c + 1) * HD] for c in range(keys // HD))
            product = jnp.dot(
                weights.astype(jnp.bfloat16), value, preferred_element_type=jnp.float32
            )
            if first:
                total[i, j] = part
                acc[i, j] = product
            else:
                total[i, j] += part
                acc[i, j] += product

    for h in range(kv_heads):
        last = h == kv_heads - 1

        def own_part(i, _):
            @pl.when(i != rank)
            def _():
                arrived(q_all.at[h, i], q_recv.at[h, i])
                if not last:
                    q_copy(h + 1, i).start()

            odd = lax.rem(i, 2)
            block(h, i, size + i, 1, True)

            def step(j, _):
                block(h, i, size + odd + 2 * j, 2, False)
                return 0

            lax.fori_loop(0, lax.div(i, 2), step, 0)
            return 0

        lax.fori_loop(0, size, own_part, 0)

        def halo_part(n, _):
            i = size - 1 - n
            if not last:
                @pl.when(i != rank)
                def _():
                    kv_arrived(h + 1, i)

                forward(h + 1, i)

            @pl.when(has_prev)
            def _():
                for m, buf in enumerate((k_all, v_all)):
                    arrived(buf.at[h, i], halo_recv.at[m, h, i])

            def step(j, _):
                block(h, i, i + 2 * j, 2, False)
                return 0

            @pl.when(has_prev)
            def _():
                lax.fori_loop(0, lax.div(size + 1 - i, 2), step, 0)

            @pl.when((group == 0) & (lax.rem(i, 2) == 1))
            def _():
                block(h, i, size, 1, False)

            for j in range(share):
                row_total = jnp.sum(total[i, j], axis=1, keepdims=True)
                out_buf[h, i, :, j * HD:(j + 1) * HD] = (acc[i, j] / row_total).astype(jnp.bfloat16)

            @pl.when(i != rank)
            def _():
                out_copy(h, i).start()

            @pl.when(i == rank)
            def _():
                own_out(h).start()

            return 0

        lax.fori_loop(0, size, halo_part, 0)

    for h in range(kv_heads):
        own_out(h).wait()
        for d in range(1, size):
            peer = (rank + d) % size
            for copy in kv_copy(h, peer):
                copy.wait_send()
            q_copy(h, peer).wait_send()
            out_copy(h, peer).wait_send()
            arrived(out_ref.at[:, cols(peer * kv_heads + h, width)], out_recv.at[h, peer])

    @pl.when(has_next)
    def _():
        for h in range(kv_heads):
            for s in range(size):
                for copy in halo_copy(h, s):
                    copy.wait_send()


def shards(n_ctx, n_uly, queries, key_rows, value_rows, doc_lengths):
    size = SPAN * n_uly
    rows, q_width = queries.shape
    kv_heads = key_rows.shape[1] // size // HD
    share = q_width // key_rows.shape[1]
    dma = pltpu.SemaphoreType.DMA
    return pl.pallas_call(
        functools.partial(kernel, n_ctx, n_uly),
        out_shape=jax.ShapeDtypeStruct(queries.shape, jnp.bfloat16),
        in_specs=[pl.BlockSpec(memory_space=pltpu.SMEM)] + [pl.BlockSpec(memory_space=pl.ANY)] * 3,
        out_specs=pl.BlockSpec(memory_space=pl.ANY),
        scratch_shapes=[
            pltpu.VMEM((kv_heads, size, rows, share * HD), jnp.bfloat16),
            pltpu.VMEM((kv_heads, 2 * size, rows, HD), jnp.bfloat16),
            pltpu.VMEM((kv_heads, 2 * size, rows, HD), jnp.bfloat16),
            pltpu.VMEM((kv_heads, size, rows, share * HD), jnp.bfloat16),
            pltpu.VMEM((size, rows, HD), jnp.int32),
            pltpu.VMEM((size, share, rows, HD), jnp.float32),
            pltpu.VMEM((size, share, rows, HD), jnp.float32),
            dma((3, kv_heads)),
            dma((2, kv_heads, size)),
            dma((2, kv_heads, size)),
            dma((kv_heads, size)),
            dma((kv_heads, size)),
            dma((2, kv_heads, size)),
            dma((2, kv_heads, size)),
            dma((kv_heads, size)),
            dma((kv_heads, size)),
        ],
        compiler_params=pltpu.CompilerParams(
            collective_id=0, has_side_effects=True, vmem_limit_bytes=48 * 1024 * 1024
        ),
    )(doc_lengths, queries, key_rows, value_rows)


def solution(mesh):
    placed = (P(("ctx", "uly"), None), P(("ctx", "uly"), None), P(("ctx", "uly"), None), P())
    return jax.shard_map(
        functools.partial(shards, mesh.shape["ctx"], mesh.shape["uly"]),
        mesh=mesh, in_specs=placed, out_specs=P(("ctx", "uly"), None), check_vma=False,
    )
```

```python
import functools
import math

import jax
import jax.numpy as jnp
from jax import lax
from jax.experimental import pallas as pl
from jax.experimental.pallas import tpu as pltpu
from jax.sharding import PartitionSpec as P

HD = 128
SPAN = 2
MESH = pl.DeviceIdType.MESH
SCALE = 144.0 ** (-0.5) / 50.0
CAP = 50.0 * math.log2(math.e)


def kernel(
    n_ctx, n_uly, lens_ref, q_ref, k_ref, v_ref, out_ref,
    q_all, k_all, v_all, out_buf, starts, acc, total,
    own_sem, kv_send, kv_recv, q_send, q_recv, halo_send, halo_recv, out_send, out_recv,
):
    size = SPAN * n_uly
    groups = n_ctx // SPAN
    rows = q_ref.shape[0]
    kv_cols = k_ref.shape[1] // size
    q_cols = q_ref.shape[1] // size
    kv_heads = kv_cols // HD
    share = q_cols // kv_cols
    width = share * HD
    me = lax.axis_index("ctx") * n_uly + lax.axis_index("uly")
    group, rank = me // size, me % size
    has_next = group < groups - 1
    has_prev = group > 0

    def device(g, r):
        flat = g * size + r
        return (flat // n_uly, flat % n_uly)

    def cols(r, width):
        return pl.ds(pl.multiple_of(r * width, width), width)

    barrier = pltpu.get_barrier_semaphore()
    for d in range(1, size):
        pl.semaphore_signal(barrier, inc=1, device_id=device(group, (rank + d) % size), device_id_type=MESH)

    @pl.when(has_next)
    def _():
        pl.semaphore_signal(barrier, inc=1, device_id=device(group + 1, rank), device_id_type=MESH)

    @pl.when(has_prev)
    def _():
        pl.semaphore_signal(barrier, inc=1, device_id=device(group - 1, rank), device_id_type=MESH)

    pl.semaphore_wait(barrier, size - 1 + jnp.where(has_next, 1, 0) + jnp.where(has_prev, 1, 0))

    def kv_copy(h, peer):
        return [
            pltpu.make_async_remote_copy(
                src_ref=src.at[:, cols(peer * kv_heads + h, HD)],
                dst_ref=dst.at[h, size + rank],
                send_sem=kv_send.at[n, h, peer],
                recv_sem=kv_recv.at[n, h, rank],
                device_id=device(group, peer),
                device_id_type=MESH,
            )
            for n, (src, dst) in enumerate(((k_ref, k_all), (v_ref, v_all)))
        ]

    def q_copy(h, peer):
        return pltpu.make_async_remote_copy(
            src_ref=q_ref.at[:, cols(peer * kv_heads + h, width)],
            dst_ref=q_all.at[h, rank],
            send_sem=q_send.at[h, peer],
            recv_sem=q_recv.at[h, rank],
            device_id=device(group, peer),
            device_id_type=MESH,
        )

    def halo_copy(h, s):
        return [
            pltpu.make_async_remote_copy(
                src_ref=buf.at[h, size + s],
                dst_ref=buf.at[h, s],
                send_sem=halo_send.at[n, h, s],
                recv_sem=halo_recv.at[n, h, s],
                device_id=device(group + 1, rank),
                device_id_type=MESH,
            )
            for n, buf in enumerate((k_all, v_all))
        ]

    def out_copy(h, i):
        return pltpu.make_async_remote_copy(
            src_ref=out_buf.at[h, i],
            dst_ref=out_ref.at[:, cols(rank * kv_heads + h, width)],
            send_sem=out_send.at[h, i],
            recv_sem=out_recv.at[h, rank],
            device_id=device(group, i),
            device_id_type=MESH,
        )

    def own_out(h):
        return pltpu.make_async_copy(
            out_buf.at[h, rank], out_ref.at[:, cols(rank * kv_heads + h, width)], own_sem.at[0, h]
        )

    def arrived(dst, sem):
        pltpu.make_async_copy(dst, dst, sem).wait()

    def kv_arrived(h, source):
        for n, buf in enumerate((k_all, v_all)):
            arrived(buf.at[h, size + source], kv_recv.at[n, h, source])

    def forward(h, source):
        @pl.when(has_next)
        def _():
            for copy in halo_copy(h, source):
                copy.start()

    for d in range(1, size):
        for copy in kv_copy(0, (rank + d) % size):
            copy.start()
    for d in range(1, size):
        q_copy(0, (rank + d) % size).start()
    own = []
    for h in range(kv_heads):
        for n, (src, dst) in enumerate(((k_ref, k_all), (v_ref, v_all))):
            own.append(pltpu.make_async_copy(
                src.at[:, cols(rank * kv_heads + h, HD)], dst.at[h, size + rank], own_sem.at[n, h]
            ))
        own.append(pltpu.make_async_copy(
            q_ref.at[:, cols(rank * kv_heads + h, width)], q_all.at[h, rank], own_sem.at[2, h]
        ))
    for copy in own:
        copy.start()

    origin = (group - 1) * size * rows

    def find_starts(i, _):
        positions = group * size * rows + i * rows + lax.broadcasted_iota(jnp.int32, (rows, HD), 0)

        def next_doc(n, carry):
            begin, found = carry
            return begin + lens_ref[n], jnp.where(begin <= positions, begin, found)

        _, found = lax.fori_loop(
            0, lens_ref.shape[0], next_doc, (jnp.int32(0), jnp.zeros((rows, HD), jnp.int32))
        )
        starts[i] = found - origin
        return 0

    lax.fori_loop(0, size, find_starts, 0)

    for copy in own:
        copy.wait()
    for d in range(size):
        source = (rank + size - d) % size
        if d:
            kv_arrived(0, source)
        forward(0, source)
        if d:
            for h in range(1, kv_heads):
                for copy in kv_copy(h, (rank + d) % size):
                    copy.start()

    def block(h, i, slot, count, first):
        keys = count * rows
        begin = starts[i] - slot * rows
        begin = jnp.concatenate([begin] * (keys // HD), axis=1)
        place = lax.broadcasted_iota(jnp.int32, (rows, keys), 1)
        allowed = place >= begin
        if first:
            allowed = allowed & (place <= lax.broadcasted_iota(jnp.int32, (rows, keys), 0))
        key = k_all[h, pl.ds(slot, count)].reshape(keys, HD)
        value = v_all[h, pl.ds(slot, count)].reshape(keys, HD)
        query = jnp.concatenate([q_all[h, i, :, j * HD:(j + 1) * HD] for j in range(share)], axis=0)
        scores = lax.dot_general(
            query, key, (((1,), (1,)), ((), ())), preferred_element_type=jnp.float32
        )
        weights = jnp.exp2(jnp.tanh(scores * SCALE) * CAP)
        weights = jnp.where(jnp.concatenate([allowed] * share, axis=0), weights, 0.0)
        part = sum(weights[:, c * HD:(c + 1) * HD] for c in range(keys // HD))
        product = jnp.dot(weights.astype(jnp.bfloat16), value, preferred_element_type=jnp.float32)
        for j in range(share):
            own_rows = slice(j * rows, (j + 1) * rows)
            if first:
                total[i, j] = part[own_rows]
                acc[i, j] = product[own_rows]
            else:
                total[i, j] += part[own_rows]
                acc[i, j] += product[own_rows]

    for h in range(kv_heads):
        last = h == kv_heads - 1

        def own_part(i, _):
            @pl.when(i != rank)
            def _():
                arrived(q_all.at[h, i], q_recv.at[h, i])
                if not last:
                    q_copy(h + 1, i).start()

            odd = lax.rem(i, 2)
            block(h, i, size + i, 1, True)

            def step(j, _):
                block(h, i, size + odd + 2 * j, 2, False)
                return 0

            lax.fori_loop(0, lax.div(i, 2), step, 0)
            return 0

        lax.fori_loop(0, size, own_part, 0)

        def halo_part(n, _):
            i = size - 1 - n
            if not last:
                @pl.when(i != rank)
                def _():
                    kv_arrived(h + 1, i)

                forward(h + 1, i)

            @pl.when(has_prev)
            def _():
                for m, buf in enumerate((k_all, v_all)):
                    arrived(buf.at[h, i], halo_recv.at[m, h, i])

            def step(j, _):
                block(h, i, i + 2 * j, 2, False)
                return 0

            @pl.when(has_prev)
            def _():
                lax.fori_loop(0, lax.div(size + 1 - i, 2), step, 0)

            @pl.when((group == 0) & (lax.rem(i, 2) == 1))
            def _():
                block(h, i, size, 1, False)

            for j in range(share):
                row_total = jnp.sum(total[i, j], axis=1, keepdims=True)
                out_buf[h, i, :, j * HD:(j + 1) * HD] = (acc[i, j] / row_total).astype(jnp.bfloat16)

            @pl.when(i != rank)
            def _():
                out_copy(h, i).start()

            @pl.when(i == rank)
            def _():
                own_out(h).start()

            return 0

        lax.fori_loop(0, size, halo_part, 0)

    for h in range(kv_heads):
        own_out(h).wait()
        for d in range(1, size):
            peer = (rank + d) % size
            for copy in kv_copy(h, peer):
                copy.wait_send()
            q_copy(h, peer).wait_send()
            out_copy(h, peer).wait_send()
            arrived(out_ref.at[:, cols(peer * kv_heads + h, width)], out_recv.at[h, peer])

    @pl.when(has_next)
    def _():
        for h in range(kv_heads):
            for s in range(size):
                for copy in halo_copy(h, s):
                    copy.wait_send()


def shards(n_ctx, n_uly, queries, key_rows, value_rows, doc_lengths):
    size = SPAN * n_uly
    rows, q_width = queries.shape
    kv_heads = key_rows.shape[1] // size // HD
    share = q_width // key_rows.shape[1]
    dma = pltpu.SemaphoreType.DMA
    return pl.pallas_call(
        functools.partial(kernel, n_ctx, n_uly),
        out_shape=jax.ShapeDtypeStruct(queries.shape, jnp.bfloat16),
        in_specs=[pl.BlockSpec(memory_space=pltpu.SMEM)] + [pl.BlockSpec(memory_space=pl.ANY)] * 3,
        out_specs=pl.BlockSpec(memory_space=pl.ANY),
        scratch_shapes=[
            pltpu.VMEM((kv_heads, size, rows, share * HD), jnp.bfloat16),
            pltpu.VMEM((kv_heads, 2 * size, rows, HD), jnp.bfloat16),
            pltpu.VMEM((kv_heads, 2 * size, rows, HD), jnp.bfloat16),
            pltpu.VMEM((kv_heads, size, rows, share * HD), jnp.bfloat16),
            pltpu.VMEM((size, rows, HD), jnp.int32),
            pltpu.VMEM((size, share, rows, HD), jnp.float32),
            pltpu.VMEM((size, share, rows, HD), jnp.float32),
            dma((3, kv_heads)),
            dma((2, kv_heads, size)),
            dma((2, kv_heads, size)),
            dma((kv_heads, size)),
            dma((kv_heads, size)),
            dma((2, kv_heads, size)),
            dma((2, kv_heads, size)),
            dma((kv_heads, size)),
            dma((kv_heads, size)),
        ],
        compiler_params=pltpu.CompilerParams(
            collective_id=0, has_side_effects=True, vmem_limit_bytes=48 * 1024 * 1024
        ),
    )(doc_lengths, queries, key_rows, value_rows)


def solution(mesh):
    placed = (P(("ctx", "uly"), None), P(("ctx", "uly"), None), P(("ctx", "uly"), None), P())
    return jax.shard_map(
        functools.partial(shards, mesh.shape["ctx"], mesh.shape["uly"]),
        mesh=mesh, in_specs=placed, out_specs=P(("ctx", "uly"), None), check_vma=False,
    )
```

```python
import functools
import math

import jax
import jax.numpy as jnp
from jax import lax
from jax.experimental import pallas as pl
from jax.experimental.pallas import tpu as pltpu
from jax.sharding import PartitionSpec as P

HD = 128
SPAN = 2
MESH = pl.DeviceIdType.MESH
SCALE = 144.0 ** (-0.5) / 50.0
CAP = 50.0 * math.log2(math.e)


def kernel(
    n_ctx, n_uly, lens_ref, q_ref, k_ref, v_ref, out_ref,
    q_all, k_all, v_all, out_buf, starts, acc, total,
    own_sem, kv_send, kv_recv, q_send, q_recv, halo_send, halo_recv, out_send, out_recv,
):
    size = SPAN * n_uly
    groups = n_ctx // SPAN
    rows = q_ref.shape[0]
    kv_cols = k_ref.shape[1] // size
    q_cols = q_ref.shape[1] // size
    kv_heads = kv_cols // HD
    share = q_cols // kv_cols
    width = share * HD
    me = lax.axis_index("ctx") * n_uly + lax.axis_index("uly")
    group, rank = me // size, me % size
    has_next = group < groups - 1
    has_prev = group > 0

    def device(g, r):
        flat = g * size + r
        return (flat // n_uly, flat % n_uly)

    def cols(r, width):
        return pl.ds(pl.multiple_of(r * width, width), width)

    barrier = pltpu.get_barrier_semaphore()
    for d in range(1, size):
        pl.semaphore_signal(barrier, inc=1, device_id=device(group, (rank + d) % size), device_id_type=MESH)

    @pl.when(has_next)
    def _():
        pl.semaphore_signal(barrier, inc=1, device_id=device(group + 1, rank), device_id_type=MESH)

    @pl.when(has_prev)
    def _():
        pl.semaphore_signal(barrier, inc=1, device_id=device(group - 1, rank), device_id_type=MESH)

    pl.semaphore_wait(barrier, size - 1 + jnp.where(has_next, 1, 0) + jnp.where(has_prev, 1, 0))

    def kv_copy(h, peer):
        return [
            pltpu.make_async_remote_copy(
                src_ref=src.at[:, cols(peer * kv_heads + h, HD)],
                dst_ref=dst.at[h, size + rank],
                send_sem=kv_send.at[n, h, peer],
                recv_sem=kv_recv.at[n, h, rank],
                device_id=device(group, peer),
                device_id_type=MESH,
            )
            for n, (src, dst) in enumerate(((k_ref, k_all), (v_ref, v_all)))
        ]

    def q_copy(h, peer):
        return pltpu.make_async_remote_copy(
            src_ref=q_ref.at[:, cols(peer * kv_heads + h, width)],
            dst_ref=q_all.at[h, rank],
            send_sem=q_send.at[h, peer],
            recv_sem=q_recv.at[h, rank],
            device_id=device(group, peer),
            device_id_type=MESH,
        )

    def halo_copy(h, s):
        return [
            pltpu.make_async_remote_copy(
                src_ref=buf.at[h, size + s],
                dst_ref=buf.at[h, s],
                send_sem=halo_send.at[n, h, s],
                recv_sem=halo_recv.at[n, h, s],
                device_id=device(group + 1, rank),
                device_id_type=MESH,
            )
            for n, buf in enumerate((k_all, v_all))
        ]

    def out_copy(h, i):
        return pltpu.make_async_remote_copy(
            src_ref=out_buf.at[h, i],
            dst_ref=out_ref.at[:, cols(rank * kv_heads + h, width)],
            send_sem=out_send.at[h, i],
            recv_sem=out_recv.at[h, rank],
            device_id=device(group, i),
            device_id_type=MESH,
        )

    def own_out(h):
        return pltpu.make_async_copy(
            out_buf.at[h, rank], out_ref.at[:, cols(rank * kv_heads + h, width)], own_sem.at[0, h]
        )

    def arrived(dst, sem):
        pltpu.make_async_copy(dst, dst, sem).wait()

    def kv_arrived(h, source):
        for n, buf in enumerate((k_all, v_all)):
            arrived(buf.at[h, size + source], kv_recv.at[n, h, source])

    def forward(h, source):
        @pl.when(has_next)
        def _():
            for copy in halo_copy(h, source):
                copy.start()

    for d in range(1, size):
        for copy in kv_copy(0, (rank + d) % size):
            copy.start()
    for d in range(1, size):
        q_copy(0, (rank + d) % size).start()
    for h in range(1, kv_heads):
        for d in range(1, size):
            for copy in kv_copy(h, (rank + d) % size):
                copy.start()
    own = []
    for h in range(kv_heads):
        for n, (src, dst) in enumerate(((k_ref, k_all), (v_ref, v_all))):
            own.append(pltpu.make_async_copy(
                src.at[:, cols(rank * kv_heads + h, HD)], dst.at[h, size + rank], own_sem.at[n, h]
            ))
        own.append(pltpu.make_async_copy(
            q_ref.at[:, cols(rank * kv_heads + h, width)], q_all.at[h, rank], own_sem.at[2, h]
        ))
    for copy in own:
        copy.start()

    origin = (group - 1) * size * rows

    def find_starts(i, _):
        positions = group * size * rows + i * rows + lax.broadcasted_iota(jnp.int32, (rows, HD), 0)

        def next_doc(n, carry):
            begin, found = carry
            return begin + lens_ref[n], jnp.where(begin <= positions, begin, found)

        _, found = lax.fori_loop(
            0, lens_ref.shape[0], next_doc, (jnp.int32(0), jnp.zeros((rows, HD), jnp.int32))
        )
        starts[i] = found - origin
        return 0

    lax.fori_loop(0, size, find_starts, 0)

    for copy in own:
        copy.wait()
    for d in range(size):
        source = (rank + size - d) % size
        if d:
            kv_arrived(0, source)
        forward(0, source)

    def block(h, i, slot, count, first):
        keys = count * rows
        begin = starts[i] - slot * rows
        begin = jnp.concatenate([begin] * (keys // HD), axis=1)
        place = lax.broadcasted_iota(jnp.int32, (rows, keys), 1)
        allowed = place >= begin
        if first:
            allowed = allowed & (place <= lax.broadcasted_iota(jnp.int32, (rows, keys), 0))
        key = k_all[h, pl.ds(slot, count)].reshape(keys, HD)
        value = v_all[h, pl.ds(slot, count)].reshape(keys, HD)
        query = jnp.concatenate([q_all[h, i, :, j * HD:(j + 1) * HD] for j in range(share)], axis=0)
        scores = lax.dot_general(
            query, key, (((1,), (1,)), ((), ())), preferred_element_type=jnp.float32
        )
        weights = jnp.exp2(jnp.tanh(scores * SCALE) * CAP)
        weights = jnp.where(jnp.concatenate([allowed] * share, axis=0), weights, 0.0)
        part = sum(weights[:, c * HD:(c + 1) * HD] for c in range(keys // HD))
        product = jnp.dot(weights.astype(jnp.bfloat16), value, preferred_element_type=jnp.float32)
        for j in range(share):
            own_rows = slice(j * rows, (j + 1) * rows)
            if first:
                total[i, j] = part[own_rows]
                acc[i, j] = product[own_rows]
            else:
                total[i, j] += part[own_rows]
                acc[i, j] += product[own_rows]

    for h in range(kv_heads):
        last = h == kv_heads - 1

        def own_part(i, _):
            @pl.when(i != rank)
            def _():
                arrived(q_all.at[h, i], q_recv.at[h, i])
                if not last:
                    q_copy(h + 1, i).start()

            odd = lax.rem(i, 2)
            block(h, i, size + i, 1, True)

            def step(j, _):
                block(h, i, size + odd + 2 * j, 2, False)
                return 0

            lax.fori_loop(0, lax.div(i, 2), step, 0)
            return 0

        lax.fori_loop(0, size, own_part, 0)

        def halo_part(n, _):
            i = size - 1 - n
            if not last:
                @pl.when(i != rank)
                def _():
                    kv_arrived(h + 1, i)

                forward(h + 1, i)

            @pl.when(has_prev)
            def _():
                for m, buf in enumerate((k_all, v_all)):
                    arrived(buf.at[h, i], halo_recv.at[m, h, i])

            def step(j, _):
                block(h, i, i + 2 * j, 2, False)
                return 0

            @pl.when(has_prev)
            def _():
                lax.fori_loop(0, lax.div(size + 1 - i, 2), step, 0)

            @pl.when((group == 0) & (lax.rem(i, 2) == 1))
            def _():
                block(h, i, size, 1, False)

            for j in range(share):
                row_total = jnp.sum(total[i, j], axis=1, keepdims=True)
                out_buf[h, i, :, j * HD:(j + 1) * HD] = (acc[i, j] / row_total).astype(jnp.bfloat16)

            @pl.when(i != rank)
            def _():
                out_copy(h, i).start()

            @pl.when(i == rank)
            def _():
                own_out(h).start()

            return 0

        lax.fori_loop(0, size, halo_part, 0)

    for h in range(kv_heads):
        own_out(h).wait()
        for d in range(1, size):
            peer = (rank + d) % size
            for copy in kv_copy(h, peer):
                copy.wait_send()
            q_copy(h, peer).wait_send()
            out_copy(h, peer).wait_send()
            arrived(out_ref.at[:, cols(peer * kv_heads + h, width)], out_recv.at[h, peer])

    @pl.when(has_next)
    def _():
        for h in range(kv_heads):
            for s in range(size):
                for copy in halo_copy(h, s):
                    copy.wait_send()


def shards(n_ctx, n_uly, queries, key_rows, value_rows, doc_lengths):
    size = SPAN * n_uly
    rows, q_width = queries.shape
    kv_heads = key_rows.shape[1] // size // HD
    share = q_width // key_rows.shape[1]
    dma = pltpu.SemaphoreType.DMA
    return pl.pallas_call(
        functools.partial(kernel, n_ctx, n_uly),
        out_shape=jax.ShapeDtypeStruct(queries.shape, jnp.bfloat16),
        in_specs=[pl.BlockSpec(memory_space=pltpu.SMEM)] + [pl.BlockSpec(memory_space=pl.ANY)] * 3,
        out_specs=pl.BlockSpec(memory_space=pl.ANY),
        scratch_shapes=[
            pltpu.VMEM((kv_heads, size, rows, share * HD), jnp.bfloat16),
            pltpu.VMEM((kv_heads, 2 * size, rows, HD), jnp.bfloat16),
            pltpu.VMEM((kv_heads, 2 * size, rows, HD), jnp.bfloat16),
            pltpu.VMEM((kv_heads, size, rows, share * HD), jnp.bfloat16),
            pltpu.VMEM((size, rows, HD), jnp.int32),
            pltpu.VMEM((size, share, rows, HD), jnp.float32),
            pltpu.VMEM((size, share, rows, HD), jnp.float32),
            dma((3, kv_heads)),
            dma((2, kv_heads, size)),
            dma((2, kv_heads, size)),
            dma((kv_heads, size)),
            dma((kv_heads, size)),
            dma((2, kv_heads, size)),
            dma((2, kv_heads, size)),
            dma((kv_heads, size)),
            dma((kv_heads, size)),
        ],
        compiler_params=pltpu.CompilerParams(
            collective_id=0, has_side_effects=True, vmem_limit_bytes=48 * 1024 * 1024
        ),
    )(doc_lengths, queries, key_rows, value_rows)


def solution(mesh):
    placed = (P(("ctx", "uly"), None), P(("ctx", "uly"), None), P(("ctx", "uly"), None), P())
    return jax.shard_map(
        functools.partial(shards, mesh.shape["ctx"], mesh.shape["uly"]),
        mesh=mesh, in_specs=placed, out_specs=P(("ctx", "uly"), None), check_vma=False,
    )
```
